256 devices in a mesh: omega: 8 (over x, core), grid: 32 (over z, y).
Axes of the slice: x: 4, y: 4, z: 8, core: 2. Of those that a mesh axis runs over, the one named last changes fastest.
Arguments:
- vectors: bfloat16 [32, 8, 1024, 1024], P(None, 'omega', 'grid'), may hold values from -6 to 6
- theta_kinetic: bfloat16 [1024, 1024], replicated
- potential: float32 [1024, 1024], P('grid'), may hold values from 0.5 to 3
- phi_coef: float32 [1024], P('grid'), may hold values from 0.3 to 3
- centrifugal: float32 [1024], P('grid'), may hold values from 0.3 to 3
- coriolis: float32 [8, 1024], P('omega', 'grid'), may hold values from 0.5 to 2
- omega_values: int32 [8], P('omega'), may hold values from 0 to 6
Outputs:
- basis: float32 [32, 8, 1024, 1024], P(None, 'omega', 'grid')
- rayleigh: float32 [32, 32], replicated
The draws below stay inside these ranges and needn't reach their ends.
All inputs are finite; a program needn't handle non-finite values.
Results may differ from the reference program's by a relative error of at most 0.0044.
Values may be sent and summed in bfloat16 or wider, within the bound.
A program may use at most 128 MiB of HBM per device.

```python
import math
import jax
import jax.numpy as jnp
from jax import lax

K = 32
NTH = 1024
NPHI = 1024
JTOT = 7
OMEGAS = 8
CELLS = 8388608


def draw_theta_kinetic(key, part):
    key = jax.random.fold_in(key, 11)
    key_off, key_diag = jax.random.split(key)
    off_diag = jax.random.normal(key_off, (NTH, NTH), jnp.float32) * (0.6 / NTH ** 0.5)
    diag_vals = jax.random.uniform(key_diag, (NTH,), jnp.float32, 1.0, 3.0)
    symmetric = (off_diag + off_diag.T) * 0.7071
    row_idx = jnp.arange(NTH)[:, None]
    col_idx = jnp.arange(NTH)[None, :]
    table = jnp.where(row_idx == col_idx, diag_vals[:, None], symmetric)
    return table.astype(jnp.bfloat16)


def place_ends(array, stream_key, low, largest):
    extent = array.shape
    index_at = [jax.random.randint(jax.random.fold_in(stream_key, axis), (), 0, extent[axis]) for axis in range(len(extent))]
    array = array.at[tuple(index_at)].set(low)
    longest = extent.index(max(extent))
    index_at[longest] = (index_at[longest] + 1) % extent[longest]
    return array.at[tuple(index_at)].set(largest)


def level_of(key, dims, pieces, smallest, high):
    def one(dim, shards_of):
        draws = jax.random.uniform(jax.random.fold_in(jax.random.fold_in(key, 6), dim), (shards_of,), jnp.float32, smallest / len(pieces), high / len(pieces))
        return jnp.repeat(jnp.exp(draws), dims[dim] // shards_of).reshape((-1,) + (1,) * (len(dims) - dim - 1))

    gain = one(*pieces[0])
    for cut in pieces[1:]:
        gain = gain * one(*cut)
    return gain


def normal_values(rng, extent, width, most, shards=(), held_as=jnp.bfloat16):
    drawn = width * jax.random.normal(rng, extent, jnp.float32)
    if shards:
        drawn = drawn * level_of(rng, extent, shards, -0.22, 0.18)
    return jnp.clip(drawn, -most, most).astype(held_as)


def setup_inputs(seed: int = 0) -> dict:
    key_of = jax.random.split(jax.random.key(seed), 8)
    return {
        "vectors": normal_values(key_of[0], (K, OMEGAS, NTH, NPHI), 1.0, 6.0, ((1, 8), (2, 32))),
        "theta_kinetic": draw_theta_kinetic(jax.random.fold_in(key_of[7], 71), 0),
        "potential": jnp.clip(0.5 + 2.5 * jax.random.uniform(key_of[2], (NTH, NPHI), jnp.float32) ** level_of(key_of[2], (NTH, NPHI), ((0, 32),), -0.2, 0.2), 0.5, 3.0),
        "phi_coef": jnp.clip(jnp.exp(math.log(3.0) - 2.3025851 * jax.random.uniform(key_of[3], (NTH,), jnp.float32) ** level_of(key_of[3], (NTH,), ((0, 32),), -0.2, 0.2)), 0.3, 3.0),
        "centrifugal": jnp.clip(jnp.exp(math.log(3.0) - 2.3025851 * jax.random.uniform(key_of[4], (NTH,), jnp.float32) ** level_of(key_of[4], (NTH,), ((0, 32),), -0.2, 0.2)), 0.3, 3.0),
        "coriolis": jnp.clip(0.5 + 1.5 * jax.random.uniform(key_of[5], (OMEGAS, NTH), jnp.float32) ** level_of(key_of[5], (OMEGAS, NTH), ((0, 8), (1, 32)), -0.2, 0.2), 0.5, 2.0),
        "omega_values": place_ends(jax.random.randint(key_of[6], (OMEGAS,), 0, JTOT), jax.random.fold_in(key_of[6], 1), 0, JTOT - 1).astype(jnp.int32),
    }


def phi_table(count):
    row_idx = jnp.arange(count, dtype=jnp.int32)[:, None]
    col_idx = jnp.arange(count, dtype=jnp.int32)[None, :]
    offset = (row_idx - col_idx) % count
    parity = (1 - 2 * (offset % 2)).astype(jnp.float32)
    sine = jnp.sin(jnp.pi * offset.astype(jnp.float32) / count)
    safe = jnp.where(offset == 0, jnp.float32(1.0), sine * sine)
    off_diag = parity / (2.0 * safe)
    centre = jnp.float32((count * count + 2) / 12.0)
    table = jnp.where(offset == 0, centre, off_diag) * jnp.float32(12.0 / (count * count))
    return table.astype(jnp.bfloat16)

def reference(vectors, theta_kinetic, potential, phi_coef, centrifugal, coriolis, omega_values):
    hi = lax.Precision.HIGHEST
    jtotal = jnp.float32(JTOT * (JTOT + 1))
    omegas = omega_values.astype(jnp.float32)
    bond_scale = jnp.sqrt(jtotal - omegas * (omegas + 1.0)) / JTOT
    bond_rows = bond_scale[:, None] * coriolis
    cent_factor = (jtotal - 2.0 * omegas * omegas) / jtotal
    table = phi_table(NPHI)
    kinetic_f = theta_kinetic.astype(jnp.float32)

    def apply_block(block_idx):
        block_vec = lax.dynamic_index_in_dim(vectors, block_idx, 1, keepdims=False)
        lower_idx = jnp.maximum(block_idx - 1, 0)
        upper_idx = jnp.minimum(block_idx + 1, OMEGAS - 1)
        below_vec = lax.dynamic_index_in_dim(vectors, lower_idx, 1, keepdims=False)
        above_vec = lax.dynamic_index_in_dim(vectors, upper_idx, 1, keepdims=False)
        below_mask = (block_idx > 0).astype(jnp.float32)
        above_mask = (block_idx < OMEGAS - 1).astype(jnp.float32)
        below_bond = lax.dynamic_index_in_dim(bond_rows, lower_idx, 0, keepdims=False) * below_mask
        own_bond = lax.dynamic_index_in_dim(bond_rows, block_idx, 0, keepdims=False) * above_mask
        own_cent = lax.dynamic_index_in_dim(cent_factor, block_idx, 0, keepdims=False)
        theta_term = jnp.einsum('ij,kjp->kip', kinetic_f, block_vec.astype(jnp.float32), precision=hi).astype(jnp.bfloat16)
        phi_term = jnp.dot(block_vec.reshape(-1, NPHI).astype(jnp.float32), table.astype(jnp.float32), preferred_element_type=jnp.float32).reshape(block_vec.shape)
        phi_term = phi_term * phi_coef[None, :, None]
        diagonal_term = potential[None] + own_cent * centrifugal[None, :, None]
        work = theta_term.astype(jnp.float32) + phi_term + diagonal_term * block_vec
        work = work + own_bond[None, :, None] * above_vec + below_bond[None, :, None] * below_vec
        return work
    stacked = lax.map(apply_block, jnp.arange(OMEGAS, dtype=jnp.int32))
    work = jnp.moveaxis(stacked, 0, 1)
    vec_f = vectors.astype(jnp.float32)
    rayleigh = jnp.einsum('kbip,lbip->kl', vec_f, work, precision=hi) / CELLS
    inv_precond = 1.0 / (1.0 + potential)
    projected = jnp.einsum('kl,kbip->lbip', rayleigh, vec_f, precision=hi)
    correction = (work - projected) * inv_precond[None, None]
    gram = jnp.einsum('kbip,lbip->kl', correction, correction, precision=hi) / CELLS
    factor = jnp.linalg.cholesky(gram)
    identity = jnp.eye(K, dtype=jnp.float32)
    factor_inv = jax.scipy.linalg.solve_triangular(factor, identity, lower=True)
    basis = jnp.einsum('lk,kbip->lbip', factor_inv, correction, precision=hi)
    return (basis, rayleigh)
```

```python
import functools

import jax
import jax.numpy as jnp
import numpy as np
from jax import lax
from jax.experimental import pallas as pl
from jax.experimental.pallas import tpu as pltpu
from jax.sharding import PartitionSpec as P

JTOT = 7
CHUNKS = 4
PH = 32
HALF = 16
F32 = jnp.float32
BF16 = jnp.bfloat16
MESH = pl.DeviceIdType.MESH
HI = lax.Precision.HIGHEST
NN = (((1,), (0,)), ((), ()))
NT = (((1,), (1,)), ((), ()))
TN = (((0,), (0,)), ((), ()))


def phi_table(count):
    row_idx = np.arange(count, dtype=np.int32)[:, None]
    col_idx = np.arange(count, dtype=np.int32)[None, :]
    offset = (row_idx - col_idx) % count
    parity = (1 - 2 * (offset % 2)).astype(np.float32)
    sine = np.sin(np.float32(np.pi) * offset.astype(np.float32) / np.float32(count)).astype(np.float32)
    safe = np.where(offset == 0, np.float32(1.0), sine * sine)
    off_diag = parity / (np.float32(2.0) * safe)
    centre = np.float32((count * count + 2) / 12.0)
    table = np.where(offset == 0, centre, off_diag) * np.float32(12.0 / (count * count))
    return table.astype(jnp.bfloat16)


def dot(a, b, dims=NN):
    return lax.dot_general(a, b, dims, preferred_element_type=F32)


def exact_dot(a, b, dims=NN):
    return lax.dot_general(a, b, dims, precision=HI, preferred_element_type=F32)


def iota(shape, dim):
    return lax.broadcasted_iota(jnp.int32, shape, dim)


def two_parts(x):
    high = x.astype(BF16)
    return high, (x - high.astype(F32)).astype(BF16)


def as_column(row):
    n = row.shape[1]
    wide = jnp.broadcast_to(row, (n, n))
    return jnp.sum(jnp.where(iota((n, n), 0) == iota((n, n), 1), wide, 0.0), axis=1, keepdims=True)


def group_sums(product, inner, outer):
    rows, cols = product.shape
    kept = jnp.where(iota((rows, cols), 0) % inner == iota((rows, cols), 1) % inner, product, 0.0)
    return jnp.sum(kept.reshape(rows // inner, inner, cols), axis=1)


def lane_sums(x, inner, outer):
    lanes = x.shape[1]
    pick = (iota((lanes, outer), 0) // inner == iota((lanes, outer), 1)).astype(F32)
    return exact_dot(x, pick)


def block_diagonal(small, inner, transposed):
    n = small.shape[0]
    full = n * inner
    rows = (iota((full, n), 0) // inner == iota((full, n), 1)).astype(BF16)
    cols = (iota((n, full), 1) // inner == iota((n, full), 0)).astype(BF16)
    tall = dot(rows, small, NT if transposed else NN).astype(BF16)
    wide = dot(tall, cols)
    same = iota((full, full), 0) % inner == iota((full, full), 1) % inner
    return jnp.where(same, wide, 0.0).astype(BF16)


def pack(x):
    return jnp.concatenate([x[8 * a : 8 * a + 8] for a in range(4)], axis=1)


def unpack(x):
    return jnp.concatenate([x[:, 32 * a : 32 * a + 32] for a in range(4)], axis=0)


def main_kernel(
    sizes,
    v_in, t_in, tab_in, pot_in, pc_in, cf_in, co_in, om_in,
    corr_out, gram_out, ray_out,
    vv, tt, tab, pot, pc, cf, co, om,
    perm, send, cols, prod, back, below, above, bond, bond_below, diag, inv, work, racc,
    ar_w, ar_y, ar_z,
    v_sem, in_sem, fs_sem, fr_sem, bs_sem, br_sem, ns_sem, nr_sem, as_sem, ar_sem, out_sem,
):
    nw, ng, ny, nz, cells = sizes
    kk, th, nphi = vv.shape
    kc = kk // CHUNKS
    lanes = kc * PH
    tiles = nphi // 128
    w = lax.axis_index("omega")
    me = lax.axis_index("grid")
    z, y = me // ny, me % ny

    v_copies = [
        pltpu.make_async_copy(v_in.at[pl.ds(c * kc, kc)], vv.at[pl.ds(c * kc, kc)], v_sem.at[c])
        for c in range(CHUNKS)
    ]
    in_copies = [
        pltpu.make_async_copy(src, dst, in_sem.at[i])
        for i, (src, dst) in enumerate(
            ((om_in, om), (co_in, co), (pc_in, pc), (cf_in, cf), (pot_in, pot), (tab_in, tab), (t_in, tt))
        )
    ]
    for copy in v_copies + in_copies:
        copy.start()

    def grid_peer(i):
        return lax.rem(z + i // ny, nz) * ny + lax.rem(y + i % ny, ny)

    barrier = pltpu.get_barrier_semaphore()

    def greet(i, carry):
        pl.semaphore_signal(barrier, inc=1, device_id={"grid": grid_peer(i), "omega": w}, device_id_type=MESH)
        return carry

    lax.fori_loop(1, ng, greet, 0)
    for i in range(1, nw):
        pl.semaphore_signal(
            barrier, inc=1, device_id={"grid": me, "omega": lax.rem(w + i, nw)}, device_id_type=MESH
        )

    source = iota((512, 512), 0)
    target = (source // PH) % 4 * 128 + source // 128 * PH + source % PH
    perm[...] = (target == iota((512, 512), 1)).astype(BF16)

    def to_columns(c):
        spots = [(q, t) for q in range(2) for t in range(tiles)]
        block = vv[pl.ds(c * kc, kc)]
        left = jnp.concatenate(
            [
                jnp.concatenate([block[4 * q + a, :, 128 * t : 128 * t + 128] for a in range(4)], axis=1)
                for q, t in spots
            ],
            axis=0,
        )
        moved = dot(left, perm[...]).astype(BF16)
        for n, (q, t) in enumerate(spots):
            for s in range(4):
                send[c, 4 * t + s, :, 128 * q : 128 * q + 128] = moved[n * th : n * th + th, 128 * s : 128 * s + 128]

    def scatter(c, src, dst, send_sem, recv_sem):
        def one(i, carry):
            peer = grid_peer(i)
            pltpu.make_async_remote_copy(
                src_ref=src.at[c, peer],
                dst_ref=dst.at[c, me],
                send_sem=send_sem.at[c],
                recv_sem=recv_sem.at[c],
                device_id={"grid": peer, "omega": w},
                device_id_type=MESH,
            ).start()
            return carry

        lax.fori_loop(1, ng, one, 0)
        dst[c, me] = src[c, me]

    def wait_all(buf, c, sem):
        rest = buf.at[c, pl.ds(0, ng - 1)]
        pltpu.make_async_copy(rest, rest, sem.at[c]).wait()

    v_copies[0].wait()
    to_columns(0)
    pl.semaphore_wait(barrier, ng - 1 + nw - 1)
    scatter(0, send, cols, fs_sem, fr_sem)
    for c in range(1, CHUNKS):
        v_copies[c].wait()

    def next_chunk(c, carry):
        to_columns(c)
        scatter(c, send, cols, fs_sem, fr_sem)
        return carry

    lax.fori_loop(1, CHUNKS, next_chunk, 0)

    for copy in in_copies:
        copy.wait()
    jtotal = F32(JTOT * (JTOT + 1))
    omega = om[...].astype(F32)
    bond_scale = jnp.sqrt(jtotal - omega * (omega + 1.0)) / JTOT
    cent_factor = (jtotal - 2.0 * omega * omega) / jtotal
    bond[...] = jnp.broadcast_to(as_column(co[...]) * bond_scale, (th, 128))
    up = {"grid": me, "omega": lax.rem(w + 1, nw)}
    down = {"grid": me, "omega": lax.rem(w + nw - 1, nw)}
    sides = [
        pltpu.make_async_remote_copy(
            src_ref=src, dst_ref=dst, send_sem=ns_sem.at[i], recv_sem=nr_sem.at[i], device_id=to, device_id_type=MESH
        )
        for i, (src, dst, to) in enumerate(((vv, below, up), (vv, above, down), (bond, bond_below, up)))
    ]
    for copy in sides:
        copy.start()

    diag[...] = pot[...] + cent_factor * as_column(cf[...])
    inv[...] = 1.0 / (1.0 + pot[...])
    phi_scale = as_column(pc[...])
    wide = min(256, nphi)

    def local_terms(i, carry):
        ks = pl.ds(i // (nphi // wide) * kc, kc)
        ps = pl.ds(pl.multiple_of(i % (nphi // wide) * wide, wide), wide)
        term = dot(vv[ks].reshape(kc * th, nphi), tab[:, ps]).reshape(kc, th, wide)
        work[ks, :, ps] = term * phi_scale[None] + diag[:, ps][None] * vv[ks, :, ps].astype(F32)
        return carry

    lax.fori_loop(0, CHUNKS * (nphi // wide), local_terms, 0)

    def theta_product(c):
        wait_all(cols, c, fr_sem)
        block = cols[c].reshape(ng * th, lanes)
        part = ng // 4

        def rows(i, carry):
            out = dot(tt[pl.ds(i * part * th, part * th)], block).astype(BF16)
            prod[c, pl.ds(i * part, part)] = out.reshape(part, th, lanes)
            return carry

        lax.fori_loop(0, 4, rows, 0)
        scatter(c, prod, back, bs_sem, br_sem)

    def ray_columns(c):
        def pair(i, carry):
            a = jnp.where(i <= c, c, i - c - 1)
            b = jnp.where(i <= c, i, c)
            product = dot(cols[a].reshape(ng * th, lanes), prod[b].reshape(ng * th, lanes), TN)
            racc[b, pl.ds(a * kc, kc)] = group_sums(product, PH, kc)
            return carry

        lax.fori_loop(0, 2 * c + 1, pair, 0)

    theta_product(0)
    ray_columns(0)
    theta_product(1)
    ray_columns(1)

    for copy in sides:
        copy.wait()
    above_factor = jnp.where(w < nw - 1, bond[...], 0.0)[:, :1]
    below_factor = jnp.where(w > 0, bond_below[...], 0.0)[:, :1]

    def couple(i, carry):
        ks = pl.ds(i * 4, 4)
        work[ks] = work[ks] + above_factor[None] * above[ks].astype(F32) + below_factor[None] * below[ks].astype(F32)
        return carry

    lax.fori_loop(0, kk // 4, couple, 0)

    theta_product(2)
    ray_columns(2)

    ray = jnp.zeros((kk, kk), F32)
    for h in range(th // HALF):
        rows = pl.ds(h * HALF, HALF)
        left = vv[:, rows].reshape(kk * HALF, nphi)
        high, low = two_parts(work[:, rows].reshape(kk * HALF, nphi))
        ray = ray + lane_sums(group_sums(dot(left, high, NT) + dot(left, low, NT), HALF, kk), HALF, kk)

    theta_product(3)
    ray_columns(3)

    def all_reduce(a, value):
        stages = (
            (ar_w, nw, w, lambda i: {"grid": me, "omega": i}),
            (ar_y, ny, y, lambda i: {"grid": z * ny + i, "omega": w}),
            (ar_z, nz, z, lambda i: {"grid": i * ny + y, "omega": w}),
        )
        for s, (buf, n, mine, device) in enumerate(stages):
            buf[a, mine] = value
            for i in range(1, n):
                pltpu.make_async_remote_copy(
                    src_ref=buf.at[a, mine],
                    dst_ref=buf.at[a, mine],
                    send_sem=as_sem.at[a, s],
                    recv_sem=ar_sem.at[a, s],
                    device_id=device(lax.rem(mine + i, n)),
                    device_id_type=MESH,
                ).start()
            rest = buf.at[a, pl.ds(0, n - 1)]
            pltpu.make_async_copy(rest, rest, ar_sem.at[a, s]).wait()
            pltpu.make_async_copy(rest, rest, as_sem.at[a, s]).wait()
            value = buf[a, 0]
            for i in range(1, n):
                value = value + buf[a, i]
        return value

    ray_cols = jnp.concatenate([racc[b] for b in range(CHUNKS)], axis=1)
    ray = ray + lane_sums(ray_cols, PH, kk)
    ray = unpack(all_reduce(0, pack(ray))) / cells
    ray_out[...] = ray

    ray_high, ray_low = two_parts(ray)
    mix_high = block_diagonal(ray_high, HALF, True)
    mix_low = block_diagonal(ray_low, HALF, True)

    def project(i, carry):
        rows = pl.ds(pl.multiple_of(i // (nphi // wide) * HALF, HALF), HALF)
        ps = pl.ds(pl.multiple_of(i % (nphi // wide) * wide, wide), wide)
        right = vv[:, rows, ps].reshape(kk * HALF, wide)
        taken = (dot(mix_high, right) + dot(mix_low, right)).reshape(kk, HALF, wide)
        work[:, rows, ps] = work[:, rows, ps] - taken
        return carry

    lax.fori_loop(0, th // HALF * (nphi // wide), project, 0)

    def correct(c, carry):
        wait_all(back, c, br_sem)
        spots = [(q, t) for q in range(2) for t in range(tiles)]
        left = jnp.concatenate(
            [
                jnp.concatenate([back[c, 4 * t + s, :, 128 * q : 128 * q + 128] for s in range(4)], axis=1)
                for q, t in spots
            ],
            axis=0,
        )
        theta = dot(left, perm[...])
        for n, (q, t) in enumerate(spots):
            ps = slice(128 * t, 128 * t + 128)
            for a in range(4):
                k = c * kc + 4 * q + a
                term = theta[n * th : n * th + th, 128 * a : 128 * a + 128]
                work[k, :, ps] = (work[k, :, ps] + term) * inv[:, ps]
        return carry

    lax.fori_loop(0, CHUNKS, correct, 0)

    out_copy = pltpu.make_async_copy(work, corr_out, out_sem)
    out_copy.start()

    gram = jnp.zeros((kk * 8, kk * 8), F32)
    for g in range(th // 8):
        high, low = two_parts(work[:, pl.ds(g * 8, 8)].reshape(kk * 8, nphi))
        gram = gram + dot(high, high, NT) + dot(high, low, NT) + dot(low, high, NT)
    gram = lane_sums(group_sums(gram, 8, kk), 8, kk)
    gram_out[...] = unpack(all_reduce(1, pack(gram))) / cells

    for c in range(CHUNKS):
        wait_all(send, c, fs_sem)
        wait_all(prod, c, bs_sem)
    out_copy.wait()


def basis_kernel(corr_in, gram_in, ray_in, basis_out, ray_out, corr, out, in_sem, out_sem):
    kk, th, nphi = corr.shape
    groups = th // 8
    rows = [pl.ds(8 * g, 8) for g in range(groups)]
    reads = [pltpu.make_async_copy(corr_in.at[:, rows[g]], corr.at[:, rows[g]], in_sem.at[g]) for g in range(groups)]
    writes = [pltpu.make_async_copy(out.at[:, rows[g]], basis_out.at[:, rows[g]], out_sem.at[g]) for g in range(groups)]
    for copy in reads:
        copy.start()
    ray_out[...] = ray_in[...]

    unit = (iota((kk, kk), 0) == iota((kk, kk), 1)).astype(F32)
    table = jnp.concatenate([gram_in[...], unit], axis=1)
    below = iota((kk, 1), 0)
    for j in range(kk - 1):
        pivot = table[j : j + 1]
        factor = jnp.where(below > j, table[:, j : j + 1] / pivot[:, j : j + 1], 0.0)
        table = table - factor * pivot
    scale = jnp.sum(table[:, :kk] * unit, axis=1, keepdims=True)
    factor_inv = table[:, kk:] / jnp.sqrt(scale)

    inv_high, inv_low = two_parts(factor_inv)
    mix_high = block_diagonal(inv_high, 8, False)
    mix_low = block_diagonal(inv_low, 8, False)
    for g in range(groups):
        reads[g].wait()
        high, low = two_parts(corr[:, rows[g]].reshape(kk * 8, nphi))
        res = dot(mix_high, high) + dot(mix_high, low) + dot(mix_low, high)
        out[:, rows[g]] = res.reshape(kk, 8, nphi)
        writes[g].start()
    for copy in writes:
        copy.wait()


def body(vectors, theta_kinetic, potential, phi_coef, centrifugal, coriolis, omega_values):
    kk, _, th, nphi = vectors.shape
    nth = theta_kinetic.shape[0]
    nw, ng = lax.axis_size("omega"), lax.axis_size("grid")
    ny = 4 if ng % 16 == 0 else 2
    nz = ng // ny
    kc = kk // CHUNKS
    cells = nw * nth * nphi
    lanes = kc * PH
    dma = pltpu.SemaphoreType.DMA
    vmem = pltpu.VMEM
    anywhere = pl.BlockSpec(memory_space=pl.ANY)
    local = pl.BlockSpec(memory_space=pltpu.VMEM)
    small = jax.ShapeDtypeStruct((kk, kk), F32)
    blocks = (CHUNKS, ng, th, lanes)
    corr, gram, rayleigh = pl.pallas_call(
        functools.partial(main_kernel, (nw, ng, ny, nz, cells)),
        out_shape=(jax.ShapeDtypeStruct((kk, th, nphi), F32), small, small),
        in_specs=[anywhere] * 8,
        out_specs=(anywhere, local, local),
        scratch_shapes=[
            vmem((kk, th, nphi), BF16), vmem((nth, nth), BF16), vmem((nphi, nphi), BF16), vmem((th, nphi), F32),
            vmem((1, th), F32), vmem((1, th), F32), vmem((1, th), F32), vmem((1, 1), jnp.int32),
            vmem((512, 512), BF16),
            vmem(blocks, BF16), vmem(blocks, BF16), vmem(blocks, BF16), vmem(blocks, BF16),
            vmem((kk, th, nphi), BF16), vmem((kk, th, nphi), BF16),
            vmem((th, 128), F32), vmem((th, 128), F32),
            vmem((th, nphi), F32), vmem((th, nphi), F32),
            vmem((kk, th, nphi), F32),
            vmem((CHUNKS, kk, lanes), F32),
            vmem((2, nw, 8, 128), F32), vmem((2, ny, 8, 128), F32), vmem((2, nz, 8, 128), F32),
            dma((CHUNKS,)), dma((7,)),
            dma((CHUNKS,)), dma((CHUNKS,)), dma((CHUNKS,)), dma((CHUNKS,)),
            dma((3,)), dma((3,)), dma((2, 3)), dma((2, 3)), dma,
        ],
        compiler_params=pltpu.CompilerParams(
            collective_id=0, has_side_effects=True, vmem_limit_bytes=48 * 1024 * 1024
        ),
    )(
        vectors.reshape(kk, th, nphi),
        theta_kinetic,
        jnp.asarray(phi_table(nphi)),
        potential,
        phi_coef.reshape(1, th),
        centrifugal.reshape(1, th),
        coriolis.reshape(1, th),
        omega_values.reshape(1, 1),
    )
    basis, rayleigh = pl.pallas_call(
        basis_kernel,
        out_shape=(jax.ShapeDtypeStruct((kk, th, nphi), F32), small),
        in_specs=[anywhere, local, local],
        out_specs=(anywhere, local),
        scratch_shapes=[vmem((kk, th, nphi), F32), vmem((kk, th, nphi), F32), dma((th // 8,)), dma((th // 8,))],
        compiler_params=pltpu.CompilerParams(vmem_limit_bytes=32 * 1024 * 1024),
    )(corr, gram, rayleigh)
    return basis.reshape(vectors.shape), rayleigh


def solution(mesh):
    placed = (
        P(None, "omega", "grid", None),
        P(),
        P("grid", None),
        P("grid"),
        P("grid"),
        P("omega", "grid"),
        P("omega"),
    )
    return jax.shard_map(
        body,
        mesh=mesh,
        in_specs=placed,
        out_specs=(P(None, "omega", "grid", None), P()),
        check_vma=False,
    )
```

```python
import functools

import jax
import jax.numpy as jnp
import numpy as np
from jax import lax
from jax.experimental import pallas as pl
from jax.experimental.pallas import tpu as pltpu
from jax.sharding import PartitionSpec as P

JTOT = 7
CHUNKS = 4
PH = 32
HALF = 16
F32 = jnp.float32
BF16 = jnp.bfloat16
MESH = pl.DeviceIdType.MESH
HI = lax.Precision.HIGHEST
NN = (((1,), (0,)), ((), ()))
NT = (((1,), (1,)), ((), ()))
TN = (((0,), (0,)), ((), ()))


def phi_table(count):
    row_idx = np.arange(count, dtype=np.int32)[:, None]
    col_idx = np.arange(count, dtype=np.int32)[None, :]
    offset = (row_idx - col_idx) % count
    parity = (1 - 2 * (offset % 2)).astype(np.float32)
    sine = np.sin(np.float32(np.pi) * offset.astype(np.float32) / np.float32(count)).astype(np.float32)
    safe = np.where(offset == 0, np.float32(1.0), sine * sine)
    off_diag = parity / (np.float32(2.0) * safe)
    centre = np.float32((count * count + 2) / 12.0)
    table = np.where(offset == 0, centre, off_diag) * np.float32(12.0 / (count * count))
    return table.astype(jnp.bfloat16)


def dot(a, b, dims=NN):
    return lax.dot_general(a, b, dims, preferred_element_type=F32)


def exact_dot(a, b, dims=NN):
    return lax.dot_general(a, b, dims, precision=HI, preferred_element_type=F32)


def iota(shape, dim):
    return lax.broadcasted_iota(jnp.int32, shape, dim)


def two_parts(x):
    high = x.astype(BF16)
    return high, (x - high.astype(F32)).astype(BF16)


def as_column(row):
    n = row.shape[1]
    wide = jnp.broadcast_to(row, (n, n))
    return jnp.sum(jnp.where(iota((n, n), 0) == iota((n, n), 1), wide, 0.0), axis=1, keepdims=True)


def group_sums(product, inner, outer):
    rows, cols = product.shape
    kept = jnp.where(iota((rows, cols), 0) % inner == iota((rows, cols), 1) % inner, product, 0.0)
    return jnp.sum(kept.reshape(rows // inner, inner, cols), axis=1)


def lane_sums(x, inner, outer):
    lanes = x.shape[1]
    pick = (iota((lanes, outer), 0) // inner == iota((lanes, outer), 1)).astype(F32)
    return exact_dot(x, pick)


def block_diagonal(small, inner, transposed):
    n = small.shape[0]
    full = n * inner
    rows = (iota((full, n), 0) // inner == iota((full, n), 1)).astype(BF16)
    cols = (iota((n, full), 1) // inner == iota((n, full), 0)).astype(BF16)
    tall = dot(rows, small, NT if transposed else NN).astype(BF16)
    wide = dot(tall, cols)
    same = iota((full, full), 0) % inner == iota((full, full), 1) % inner
    return jnp.where(same, wide, 0.0).astype(BF16)


def pack(x):
    return jnp.concatenate([x[8 * a : 8 * a + 8] for a in range(4)], axis=1)


def unpack(x):
    return jnp.concatenate([x[:, 32 * a : 32 * a + 32] for a in range(4)], axis=0)


def main_kernel(
    sizes,
    v_in, t_in, tab_in, pot_in, pc_in, cf_in, co_in, om_in,
    high_out, low_out, gram_out, ray_out,
    vv, tt, tab, pot, pc, cf, co, om,
    perm, send, cols, prod, back, below, above, bond, bond_below, diag, inv, work, racc, high, low,
    ar_wy, ar_z,
    v_sem, in_sem, fs_sem, fr_sem, bs_sem, br_sem, ns_sem, nr_sem, as_sem, ar_sem, out_sem,
):
    nw, ng, ny, nz, cells = sizes
    kk, th, nphi = vv.shape
    kc = kk // CHUNKS
    lanes = kc * PH
    tiles = nphi // 128
    w = lax.axis_index("omega")
    me = lax.axis_index("grid")
    z, y = me // ny, me % ny

    v_copies = [
        pltpu.make_async_copy(v_in.at[pl.ds(c * kc, kc)], vv.at[pl.ds(c * kc, kc)], v_sem.at[c])
        for c in range(CHUNKS)
    ]
    in_copies = [
        pltpu.make_async_copy(src, dst, in_sem.at[i])
        for i, (src, dst) in enumerate(
            ((om_in, om), (co_in, co), (pc_in, pc), (cf_in, cf), (pot_in, pot), (tab_in, tab), (t_in, tt))
        )
    ]
    for copy in v_copies + in_copies:
        copy.start()

    def grid_peer(i):
        return lax.rem(z + i // ny, nz) * ny + lax.rem(y + i % ny, ny)

    barrier = pltpu.get_barrier_semaphore()

    def greet(i, carry):
        pl.semaphore_signal(barrier, inc=1, device_id={"grid": grid_peer(i), "omega": w}, device_id_type=MESH)
        return carry

    lax.fori_loop(1, ng, greet, 0)
    def greet_beside(i, carry):
        peer = {"grid": z * ny + i % ny, "omega": lax.rem(w + i // ny, nw)}
        pl.semaphore_signal(barrier, inc=1, device_id=peer, device_id_type=MESH)
        return carry

    lax.fori_loop(ny, nw * ny, greet_beside, 0)

    source = iota((512, 512), 0)
    target = (source // PH) % 4 * 128 + source // 128 * PH + source % PH
    perm[...] = (target == iota((512, 512), 1)).astype(BF16)

    def to_columns(c):
        spots = [(q, t) for q in range(2) for t in range(tiles)]
        block = vv[pl.ds(c * kc, kc)]
        left = jnp.concatenate(
            [
                jnp.concatenate([block[4 * q + a, :, 128 * t : 128 * t + 128] for a in range(4)], axis=1)
                for q, t in spots
            ],
            axis=0,
        )
        moved = dot(left, perm[...]).astype(BF16)
        for n, (q, t) in enumerate(spots):
            for s in range(4):
                send[c, 4 * t + s, :, 128 * q : 128 * q + 128] = moved[n * th : n * th + th, 128 * s : 128 * s + 128]

    def scatter(c, src, dst, send_sem, recv_sem):
        def one(i, carry):
            peer = grid_peer(i)
            pltpu.make_async_remote_copy(
                src_ref=src.at[c, peer],
                dst_ref=dst.at[c, me],
                send_sem=send_sem.at[c],
                recv_sem=recv_sem.at[c],
                device_id={"grid": peer, "omega": w},
                device_id_type=MESH,
            ).start()
            return carry

        lax.fori_loop(1, ng, one, 0)
        dst[c, me] = src[c, me]

    def wait_all(buf, c, sem):
        rest = buf.at[c, pl.ds(0, ng - 1)]
        pltpu.make_async_copy(rest, rest, sem.at[c]).wait()

    v_copies[0].wait()
    to_columns(0)
    pl.semaphore_wait(barrier, ng - 1 + (nw - 1) * ny)
    scatter(0, send, cols, fs_sem, fr_sem)
    for c in range(1, CHUNKS):
        v_copies[c].wait()

    def next_chunk(c, carry):
        to_columns(c)
        scatter(c, send, cols, fs_sem, fr_sem)
        return carry

    lax.fori_loop(1, CHUNKS, next_chunk, 0)

    for copy in in_copies:
        copy.wait()
    jtotal = F32(JTOT * (JTOT + 1))
    omega = om[...].astype(F32)
    bond_scale = jnp.sqrt(jtotal - omega * (omega + 1.0)) / JTOT
    cent_factor = (jtotal - 2.0 * omega * omega) / jtotal
    bond[...] = jnp.broadcast_to(as_column(co[...]) * bond_scale, (th, 128))
    up = {"grid": me, "omega": lax.rem(w + 1, nw)}
    down = {"grid": me, "omega": lax.rem(w + nw - 1, nw)}
    sides = [
        pltpu.make_async_remote_copy(
            src_ref=src, dst_ref=dst, send_sem=ns_sem.at[i], recv_sem=nr_sem.at[i], device_id=to, device_id_type=MESH
        )
        for i, (src, dst, to) in enumerate(((vv, below, up), (vv, above, down), (bond, bond_below, up)))
    ]
    for copy in sides:
        copy.start()

    diag[...] = pot[...] + cent_factor * as_column(cf[...])
    inv[...] = 1.0 / (1.0 + pot[...])
    phi_scale = as_column(pc[...])
    wide = min(256, nphi)

    def local_terms(i, carry):
        ks = pl.ds(i // (nphi // wide) * kc, kc)
        ps = pl.ds(pl.multiple_of(i % (nphi // wide) * wide, wide), wide)
        term = dot(vv[ks].reshape(kc * th, nphi), tab[:, ps]).reshape(kc, th, wide)
        work[ks, :, ps] = term * phi_scale[None] + diag[:, ps][None] * vv[ks, :, ps].astype(F32)
        return carry

    lax.fori_loop(0, CHUNKS * (nphi // wide), local_terms, 0)

    def theta_product(c):
        wait_all(cols, c, fr_sem)
        block = cols[c].reshape(ng * th, lanes)
        part = ng // 4

        def rows(i, carry):
            out = dot(tt[pl.ds(i * part * th, part * th)], block).astype(BF16)
            prod[c, pl.ds(i * part, part)] = out.reshape(part, th, lanes)
            return carry

        lax.fori_loop(0, 4, rows, 0)

    def ray_columns(c):
        def pair(i, carry):
            a = jnp.where(i <= c, c, i - c - 1)
            b = jnp.where(i <= c, i, c)
            product = dot(cols[a].reshape(ng * th, lanes), prod[b].reshape(ng * th, lanes), TN)
            racc[b, pl.ds(a * kc, kc)] = group_sums(product, PH, kc)
            return carry

        lax.fori_loop(0, 2 * c + 1, pair, 0)

    theta_product(0)
    scatter(0, prod, back, bs_sem, br_sem)
    ray_columns(0)
    theta_product(1)
    ray_columns(1)

    for copy in sides:
        copy.wait()
    above_factor = jnp.where(w < nw - 1, bond[...], 0.0)[:, :1]
    below_factor = jnp.where(w > 0, bond_below[...], 0.0)[:, :1]

    def couple(i, carry):
        ks = pl.ds(i * 4, 4)
        work[ks] = work[ks] + above_factor[None] * above[ks].astype(F32) + below_factor[None] * below[ks].astype(F32)
        return carry

    lax.fori_loop(0, kk // 4, couple, 0)

    theta_product(2)
    ray_columns(2)

    ray = jnp.zeros((kk, kk), F32)
    for h in range(th // HALF):
        rows = pl.ds(h * HALF, HALF)
        left = vv[:, rows].reshape(kk * HALF, nphi)
        x, x_rest = two_parts(work[:, rows].reshape(kk * HALF, nphi))
        ray = ray + lane_sums(group_sums(dot(left, x, NT) + dot(left, x_rest, NT), HALF, kk), HALF, kk)

    theta_product(3)
    ray_columns(3)

    stages = (
        (ar_wy, nw * ny, w * ny + y, lambda i: {"grid": z * ny + i % ny, "omega": i // ny}),
        (ar_z, nz, z, lambda i: {"grid": i * ny + y, "omega": w}),
    )

    def share(a, s, value):
        buf, n, mine, device = stages[s]
        buf[a, mine] = value

        def one(i, carry):
            pltpu.make_async_remote_copy(
                src_ref=buf.at[a, mine],
                dst_ref=buf.at[a, mine],
                send_sem=as_sem.at[a, s],
                recv_sem=ar_sem.at[a, s],
                device_id=device(lax.rem(mine + i, n)),
                device_id_type=MESH,
            ).start()
            return carry

        lax.fori_loop(1, n, one, 0)

    def total(a, s):
        buf, n, _, _ = stages[s]
        rest = buf.at[a, pl.ds(0, n - 1)]
        pltpu.make_async_copy(rest, rest, ar_sem.at[a, s]).wait()
        pltpu.make_async_copy(rest, rest, as_sem.at[a, s]).wait()
        return jnp.sum(buf[a], axis=0)

    ray_cols = jnp.concatenate([racc[b] for b in range(CHUNKS)], axis=1)
    ray = ray + lane_sums(ray_cols, PH, kk)
    share(0, 0, pack(ray))
    scatter(1, prod, back, bs_sem, br_sem)
    share(0, 1, total(0, 0))
    scatter(2, prod, back, bs_sem, br_sem)
    ray = unpack(total(0, 1)) / cells
    scatter(3, prod, back, bs_sem, br_sem)
    ray_out[...] = ray

    ray_high, ray_low = two_parts(ray)
    mix_high = block_diagonal(ray_high, HALF, True)
    mix_low = block_diagonal(ray_low, HALF, True)

    def project(i, carry):
        rows = pl.ds(pl.multiple_of(i // (nphi // wide) * HALF, HALF), HALF)
        ps = pl.ds(pl.multiple_of(i % (nphi // wide) * wide, wide), wide)
        right = vv[:, rows, ps].reshape(kk * HALF, wide)
        taken = (dot(mix_high, right) + dot(mix_low, right)).reshape(kk, HALF, wide)
        work[:, rows, ps] = work[:, rows, ps] - taken
        return carry

    lax.fori_loop(0, th // HALF * (nphi // wide), project, 0)

    def correct(c, carry):
        wait_all(back, c, br_sem)
        spots = [(q, t) for q in range(2) for t in range(tiles)]
        left = jnp.concatenate(
            [
                jnp.concatenate([back[c, 4 * t + s, :, 128 * q : 128 * q + 128] for s in range(4)], axis=1)
                for q, t in spots
            ],
            axis=0,
        )
        theta = dot(left, perm[...])
        for n, (q, t) in enumerate(spots):
            ps = slice(128 * t, 128 * t + 128)
            for a in range(4):
                k = c * kc + 4 * q + a
                term = theta[n * th : n * th + th, 128 * a : 128 * a + 128]
                work[k, :, ps] = (work[k, :, ps] + term) * inv[:, ps]
        return carry

    lax.fori_loop(0, CHUNKS, correct, 0)

    gram = jnp.zeros((kk * 8, kk * 8), F32)
    cross = jnp.zeros((kk * 8, kk * 8), F32)
    out_copies = []
    for g in range(th // 8):
        x, x_rest = two_parts(work[:, pl.ds(g * 8, 8)].reshape(kk * 8, nphi))
        high[g] = x
        low[g] = x_rest
        gram = gram + dot(x, x, NT)
        cross = cross + dot(x, x_rest, NT)
        out_copies.append(pltpu.make_async_copy(high.at[g], high_out.at[g], out_sem.at[0, g]))
        out_copies.append(pltpu.make_async_copy(low.at[g], low_out.at[g], out_sem.at[1, g]))
        out_copies[-2].start()
        out_copies[-1].start()
    gram = lane_sums(group_sums(gram, 8, kk), 8, kk)
    cross = lane_sums(group_sums(cross, 8, kk), 8, kk)
    unit = (iota((kk, kk), 0) == iota((kk, kk), 1)).astype(F32)
    gram = gram + cross + exact_dot(unit, cross, NT)
    share(1, 0, pack(gram))
    share(1, 1, total(1, 0))
    gram_out[...] = unpack(total(1, 1)) / cells

    for c in range(CHUNKS):
        wait_all(send, c, fs_sem)
        wait_all(prod, c, bs_sem)
    for copy in out_copies:
        copy.wait()


def basis_kernel(high_in, low_in, gram_in, ray_in, basis_out, ray_out, high, low, out, in_sem, out_sem):
    groups, rows, nphi = high.shape
    kk = rows // 8
    reads = [
        pltpu.make_async_copy(src.at[g], dst.at[g], in_sem.at[i, g])
        for g in range(groups)
        for i, (src, dst) in enumerate(((high_in, high), (low_in, low)))
    ]
    part = [pl.ds(8 * g, 8) for g in range(groups)]
    writes = [pltpu.make_async_copy(out.at[:, part[g]], basis_out.at[:, part[g]], out_sem.at[g]) for g in range(groups)]
    for copy in reads:
        copy.start()
    ray_out[...] = ray_in[...]

    unit = (iota((kk, kk), 0) == iota((kk, kk), 1)).astype(F32)
    table = jnp.concatenate([gram_in[...], unit], axis=1)
    row = iota(table.shape, 0)
    for first in range(0, kk, 4):
        spread = [jnp.broadcast_to(table[:, j : j + 1], table.shape) for j in range(first, first + 4)]
        for a in range(4):
            j = first + a
            factor = jnp.where(row > j, spread[a] * (1.0 / spread[a][j : j + 1]), 0.0)
            for b in range(a + 1, 4):
                spread[b] = spread[b] - factor * spread[b][j : j + 1]
            table = table - factor * table[j : j + 1]
    scale = jnp.sum(table[:, :kk] * unit, axis=1, keepdims=True)
    factor_inv = table[:, kk:] / jnp.sqrt(scale)

    inv_high, inv_low = two_parts(factor_inv)
    mix_high = block_diagonal(inv_high, 8, False)
    mix_low = block_diagonal(inv_low, 8, False)
    for g in range(groups):
        reads[2 * g].wait()
        reads[2 * g + 1].wait()
        x = high[g]
        res = dot(mix_high, x) + dot(mix_high, low[g]) + dot(mix_low, x)
        out[:, part[g]] = res.reshape(kk, 8, nphi)
        writes[g].start()
    for copy in writes:
        copy.wait()


def body(vectors, theta_kinetic, potential, phi_coef, centrifugal, coriolis, omega_values):
    kk, _, th, nphi = vectors.shape
    nth = theta_kinetic.shape[0]
    nw, ng = lax.axis_size("omega"), lax.axis_size("grid")
    ny = 4 if ng % 16 == 0 else 2
    nz = ng // ny
    kc = kk // CHUNKS
    cells = nw * nth * nphi
    lanes = kc * PH
    dma = pltpu.SemaphoreType.DMA
    vmem = pltpu.VMEM
    anywhere = pl.BlockSpec(memory_space=pl.ANY)
    local = pl.BlockSpec(memory_space=pltpu.VMEM)
    small = jax.ShapeDtypeStruct((kk, kk), F32)
    blocks = (CHUNKS, ng, th, lanes)
    split = jax.ShapeDtypeStruct((th // 8, kk * 8, nphi), BF16)
    high, low, gram, rayleigh = pl.pallas_call(
        functools.partial(main_kernel, (nw, ng, ny, nz, cells)),
        out_shape=(split, split, small, small),
        in_specs=[anywhere] * 8,
        out_specs=(anywhere, anywhere, local, local),
        scratch_shapes=[
            vmem((kk, th, nphi), BF16), vmem((nth, nth), BF16), vmem((nphi, nphi), BF16), vmem((th, nphi), F32),
            vmem((1, th), F32), vmem((1, th), F32), vmem((1, th), F32), vmem((1, 1), jnp.int32),
            vmem((512, 512), BF16),
            vmem(blocks, BF16), vmem(blocks, BF16), vmem(blocks, BF16), vmem(blocks, BF16),
            vmem((kk, th, nphi), BF16), vmem((kk, th, nphi), BF16),
            vmem((th, 128), F32), vmem((th, 128), F32),
            vmem((th, nphi), F32), vmem((th, nphi), F32),
            vmem((kk, th, nphi), F32),
            vmem((CHUNKS, kk, lanes), F32),
            vmem(split.shape, BF16), vmem(split.shape, BF16),
            vmem((2, nw * ny, 8, 128), F32), vmem((2, nz, 8, 128), F32),
            dma((CHUNKS,)), dma((7,)),
            dma((CHUNKS,)), dma((CHUNKS,)), dma((CHUNKS,)), dma((CHUNKS,)),
            dma((3,)), dma((3,)), dma((2, 2)), dma((2, 2)), dma((2, th // 8)),
        ],
        compiler_params=pltpu.CompilerParams(
            collective_id=0, has_side_effects=True, vmem_limit_bytes=62 * 1024 * 1024
        ),
    )(
        vectors.reshape(kk, th, nphi),
        theta_kinetic,
        jnp.asarray(phi_table(nphi)),
        potential,
        phi_coef.reshape(1, th),
        centrifugal.reshape(1, th),
        coriolis.reshape(1, th),
        omega_values.reshape(1, 1),
    )
    basis, rayleigh = pl.pallas_call(
        basis_kernel,
        out_shape=(jax.ShapeDtypeStruct((kk, th, nphi), F32), small),
        in_specs=[anywhere, anywhere, local, local],
        out_specs=(anywhere, local),
        scratch_shapes=[
            vmem(split.shape, BF16), vmem(split.shape, BF16), vmem((kk, th, nphi), F32),
            dma((2, th // 8)), dma((th // 8,)),
        ],
        compiler_params=pltpu.CompilerParams(vmem_limit_bytes=62 * 1024 * 1024),
    )(high, low, gram, rayleigh)
    return basis.reshape(vectors.shape), rayleigh


def solution(mesh):
    placed = (
        P(None, "omega", "grid", None),
        P(),
        P("grid", None),
        P("grid"),
        P("grid"),
        P("omega", "grid"),
        P("omega"),
    )
    return jax.shard_map(
        body,
        mesh=mesh,
        in_specs=placed,
        out_specs=(P(None, "omega", "grid", None), P()),
        check_vma=False,
    )
```

```python
import functools

import jax
import jax.numpy as jnp
import numpy as np
from jax import lax
from jax.experimental import pallas as pl
from jax.experimental.pallas import tpu as pltpu
from jax.sharding import PartitionSpec as P

JTOT = 7
CHUNKS = 4
PH = 32
HALF = 16
F32 = jnp.float32
BF16 = jnp.bfloat16
MESH = pl.DeviceIdType.MESH
HI = lax.Precision.HIGHEST
NN = (((1,), (0,)), ((), ()))
NT = (((1,), (1,)), ((), ()))
TN = (((0,), (0,)), ((), ()))


def phi_table(count):
    row_idx = np.arange(count, dtype=np.int32)[:, None]
    col_idx = np.arange(count, dtype=np.int32)[None, :]
    offset = (row_idx - col_idx) % count
    parity = (1 - 2 * (offset % 2)).astype(np.float32)
    sine = np.sin(np.float32(np.pi) * offset.astype(np.float32) / np.float32(count)).astype(np.float32)
    safe = np.where(offset == 0, np.float32(1.0), sine * sine)
    off_diag = parity / (np.float32(2.0) * safe)
    centre = np.float32((count * count + 2) / 12.0)
    table = np.where(offset == 0, centre, off_diag) * np.float32(12.0 / (count * count))
    return table.astype(jnp.bfloat16)


def dot(a, b, dims=NN):
    return lax.dot_general(a, b, dims, preferred_element_type=F32)


def exact_dot(a, b, dims=NN):
    return lax.dot_general(a, b, dims, precision=HI, preferred_element_type=F32)


def iota(shape, dim):
    return lax.broadcasted_iota(jnp.int32, shape, dim)


def two_parts(x):
    high = x.astype(BF16)
    return high, (x - high.astype(F32)).astype(BF16)


def as_column(row):
    n = row.shape[1]
    wide = jnp.broadcast_to(row, (n, n))
    return jnp.sum(jnp.where(iota((n, n), 0) == iota((n, n), 1), wide, 0.0), axis=1, keepdims=True)


def group_sums(product, inner, outer):
    rows, cols = product.shape
    kept = jnp.where(iota((rows, cols), 0) % inner == iota((rows, cols), 1) % inner, product, 0.0)
    return jnp.sum(kept.reshape(rows // inner, inner, cols), axis=1)


def lane_sums(x, inner, outer):
    lanes = x.shape[1]
    pick = (iota((lanes, outer), 0) // inner == iota((lanes, outer), 1)).astype(F32)
    return exact_dot(x, pick)


def block_diagonal(small, inner, transposed):
    n = small.shape[0]
    full = n * inner
    rows = (iota((full, n), 0) // inner == iota((full, n), 1)).astype(BF16)
    cols = (iota((n, full), 1) // inner == iota((n, full), 0)).astype(BF16)
    tall = dot(rows, small, NT if transposed else NN).astype(BF16)
    wide = dot(tall, cols)
    same = iota((full, full), 0) % inner == iota((full, full), 1) % inner
    return jnp.where(same, wide, 0.0).astype(BF16)


def pack(x):
    return jnp.concatenate([x[8 * a : 8 * a + 8] for a in range(4)], axis=1)


def unpack(x):
    return jnp.concatenate([x[:, 32 * a : 32 * a + 32] for a in range(4)], axis=0)


def main_kernel(
    sizes,
    v_in, t_in, tab_in, pot_in, pc_in, cf_in, co_in, om_in,
    high, low, gram_out, ray_out,
    vv, tt, tab, pot, pc, cf, co, om,
    perm, send, cols, prod, back, below, above, bond, bond_below, diag, inv, work, racc,
    ar_wy, ar_z,
    v_sem, in_sem, fs_sem, fr_sem, bs_sem, br_sem, ns_sem, nr_sem, as_sem, ar_sem,
):
    nw, ng, ny, nz, cells = sizes
    kk, th, nphi = vv.shape
    kc = kk // CHUNKS
    lanes = kc * PH
    tiles = nphi // 128
    w = lax.axis_index("omega")
    me = lax.axis_index("grid")
    z, y = me // ny, me % ny

    v_copies = [
        pltpu.make_async_copy(v_in.at[pl.ds(c * kc, kc)], vv.at[pl.ds(c * kc, kc)], v_sem.at[c])
        for c in range(CHUNKS)
    ]
    in_copies = [
        pltpu.make_async_copy(src, dst, in_sem.at[i])
        for i, (src, dst) in enumerate(
            ((om_in, om), (co_in, co), (pc_in, pc), (cf_in, cf), (pot_in, pot), (tab_in, tab), (t_in, tt))
        )
    ]
    v_copies[0].start()

    def grid_peer(i):
        return lax.rem(z + i // ny, nz) * ny + lax.rem(y + i % ny, ny)

    barrier = pltpu.get_barrier_semaphore()

    def greet(i, carry):
        pl.semaphore_signal(barrier, inc=1, device_id={"grid": grid_peer(i), "omega": w}, device_id_type=MESH)
        return carry

    lax.fori_loop(1, ng, greet, 0)
    def greet_beside(i, carry):
        peer = {"grid": z * ny + i % ny, "omega": lax.rem(w + i // ny, nw)}
        pl.semaphore_signal(barrier, inc=1, device_id=peer, device_id_type=MESH)
        return carry

    lax.fori_loop(ny, nw * ny, greet_beside, 0)

    for copy in v_copies[1:] + in_copies:
        copy.start()

    source = iota((512, 512), 0)
    target = (source // PH) % 4 * 128 + source // 128 * PH + source % PH
    perm[...] = (target == iota((512, 512), 1)).astype(BF16)

    def to_columns(c):
        spots = [(q, t) for q in range(2) for t in range(tiles)]
        block = vv[pl.ds(c * kc, kc)]
        left = jnp.concatenate(
            [
                jnp.concatenate([block[4 * q + a, :, 128 * t : 128 * t + 128] for a in range(4)], axis=1)
                for q, t in spots
            ],
            axis=0,
        )
        moved = dot(left, perm[...]).astype(BF16)
        for n, (q, t) in enumerate(spots):
            for s in range(4):
                send[c, 4 * t + s, :, 128 * q : 128 * q + 128] = moved[n * th : n * th + th, 128 * s : 128 * s + 128]

    def scatter(c, src, dst, send_sem, recv_sem):
        def one(i, carry):
            peer = grid_peer(i)
            pltpu.make_async_remote_copy(
                src_ref=src.at[c, peer],
                dst_ref=dst.at[c, me],
                send_sem=send_sem.at[c],
                recv_sem=recv_sem.at[c],
                device_id={"grid": peer, "omega": w},
                device_id_type=MESH,
            ).start()
            return carry

        lax.fori_loop(1, ng, one, 0)
        dst[c, me] = src[c, me]

    def wait_all(buf, c, sem):
        rest = buf.at[c, pl.ds(0, ng - 1)]
        pltpu.make_async_copy(rest, rest, sem.at[c]).wait()

    v_copies[0].wait()
    to_columns(0)
    pl.semaphore_wait(barrier, ng - 1 + (nw - 1) * ny)
    scatter(0, send, cols, fs_sem, fr_sem)
    for c in range(1, CHUNKS):
        v_copies[c].wait()

    def next_chunk(c, carry):
        to_columns(c)
        scatter(c, send, cols, fs_sem, fr_sem)
        return carry

    lax.fori_loop(1, CHUNKS, next_chunk, 0)

    for copy in in_copies:
        copy.wait()
    jtotal = F32(JTOT * (JTOT + 1))
    omega = om[...].astype(F32)
    bond_scale = jnp.sqrt(jtotal - omega * (omega + 1.0)) / JTOT
    cent_factor = (jtotal - 2.0 * omega * omega) / jtotal
    bond[...] = jnp.broadcast_to(as_column(co[...]) * bond_scale, (th, 128))
    up = {"grid": me, "omega": lax.rem(w + 1, nw)}
    down = {"grid": me, "omega": lax.rem(w + nw - 1, nw)}
    sides = [
        pltpu.make_async_remote_copy(
            src_ref=src, dst_ref=dst, send_sem=ns_sem.at[i], recv_sem=nr_sem.at[i], device_id=to, device_id_type=MESH
        )
        for i, (src, dst, to) in enumerate(((vv, below, up), (vv, above, down), (bond, bond_below, up)))
    ]
    for copy in sides:
        copy.start()

    diag[...] = pot[...] + cent_factor * as_column(cf[...])
    inv[...] = 1.0 / (1.0 + pot[...])
    phi_scale = as_column(pc[...])
    wide = min(256, nphi)

    def local_terms(i, carry):
        ks = pl.ds(i // (nphi // wide) * kc, kc)
        ps = pl.ds(pl.multiple_of(i % (nphi // wide) * wide, wide), wide)
        term = dot(vv[ks].reshape(kc * th, nphi), tab[:, ps]).reshape(kc, th, wide)
        work[ks, :, ps] = term * phi_scale[None] + diag[:, ps][None] * vv[ks, :, ps].astype(F32)
        return carry

    lax.fori_loop(0, CHUNKS * (nphi // wide), local_terms, 0)

    def theta_product(c):
        wait_all(cols, c, fr_sem)
        block = cols[c].reshape(ng * th, lanes)
        part = ng // 4

        def rows(i, carry):
            out = dot(tt[pl.ds(i * part * th, part * th)], block).astype(BF16)
            prod[c, pl.ds(i * part, part)] = out.reshape(part, th, lanes)
            return carry

        lax.fori_loop(0, 4, rows, 0)

    def ray_columns(c):
        def pair(i, carry):
            a = jnp.where(i <= c, c, i - c - 1)
            b = jnp.where(i <= c, i, c)
            product = dot(cols[a].reshape(ng * th, lanes), prod[b].reshape(ng * th, lanes), TN)
            racc[b, pl.ds(a * kc, kc)] = group_sums(product, PH, kc)
            return carry

        lax.fori_loop(0, 2 * c + 1, pair, 0)

    theta_product(0)
    scatter(0, prod, back, bs_sem, br_sem)
    ray_columns(0)
    theta_product(1)
    ray_columns(1)

    for copy in sides:
        copy.wait()
    above_factor = jnp.where(w < nw - 1, bond[...], 0.0)[:, :1]
    below_factor = jnp.where(w > 0, bond_below[...], 0.0)[:, :1]

    def couple(i, carry):
        ks = pl.ds(i * 4, 4)
        work[ks] = work[ks] + above_factor[None] * above[ks].astype(F32) + below_factor[None] * below[ks].astype(F32)
        return carry

    lax.fori_loop(0, kk // 4, couple, 0)

    theta_product(2)
    ray_columns(2)

    ray = jnp.zeros((kk, kk), F32)
    for h in range(th // HALF):
        rows = pl.ds(h * HALF, HALF)
        left = vv[:, rows].reshape(kk * HALF, nphi)
        x, x_rest = two_parts(work[:, rows].reshape(kk * HALF, nphi))
        ray = ray + lane_sums(group_sums(dot(left, x, NT) + dot(left, x_rest, NT), HALF, kk), HALF, kk)

    theta_product(3)
    ray_columns(3)

    stages = (
        (ar_wy, nw * ny, w * ny + y, lambda i: {"grid": z * ny + i % ny, "omega": i // ny}),
        (ar_z, nz, z, lambda i: {"grid": i * ny + y, "omega": w}),
    )

    def share(a, s, value):
        buf, n, mine, device = stages[s]
        buf[a, mine] = value

        def one(i, carry):
            pltpu.make_async_remote_copy(
                src_ref=buf.at[a, mine],
                dst_ref=buf.at[a, mine],
                send_sem=as_sem.at[a, s],
                recv_sem=ar_sem.at[a, s],
                device_id=device(lax.rem(mine + i, n)),
                device_id_type=MESH,
            ).start()
            return carry

        lax.fori_loop(1, n, one, 0)

    def total(a, s):
        buf, n, _, _ = stages[s]
        rest = buf.at[a, pl.ds(0, n - 1)]
        pltpu.make_async_copy(rest, rest, ar_sem.at[a, s]).wait()
        pltpu.make_async_copy(rest, rest, as_sem.at[a, s]).wait()
        return jnp.sum(buf[a], axis=0)

    ray_cols = jnp.concatenate([racc[b] for b in range(CHUNKS)], axis=1)
    ray = ray + lane_sums(ray_cols, PH, kk)
    share(0, 0, pack(ray))
    scatter(1, prod, back, bs_sem, br_sem)
    share(0, 1, total(0, 0))
    scatter(2, prod, back, bs_sem, br_sem)
    ray = unpack(total(0, 1)) / cells
    scatter(3, prod, back, bs_sem, br_sem)
    ray_out[...] = ray

    ray_high, ray_low = two_parts(ray)
    mix_high = block_diagonal(ray_high, HALF, True)
    mix_low = block_diagonal(ray_low, HALF, True)

    def project(i, carry):
        rows = pl.ds(pl.multiple_of(i // (nphi // wide) * HALF, HALF), HALF)
        ps = pl.ds(pl.multiple_of(i % (nphi // wide) * wide, wide), wide)
        right = vv[:, rows, ps].reshape(kk * HALF, wide)
        taken = (dot(mix_high, right) + dot(mix_low, right)).reshape(kk, HALF, wide)
        work[:, rows, ps] = work[:, rows, ps] - taken
        return carry

    lax.fori_loop(0, th // HALF * (nphi // wide), project, 0)

    def correct(c, carry):
        wait_all(back, c, br_sem)
        spots = [(q, t) for q in range(2) for t in range(tiles)]
        left = jnp.concatenate(
            [
                jnp.concatenate([back[c, 4 * t + s, :, 128 * q : 128 * q + 128] for s in range(4)], axis=1)
                for q, t in spots
            ],
            axis=0,
        )
        theta = dot(left, perm[...])
        for n, (q, t) in enumerate(spots):
            ps = slice(128 * t, 128 * t + 128)
            for a in range(4):
                k = c * kc + 4 * q + a
                term = theta[n * th : n * th + th, 128 * a : 128 * a + 128]
                work[k, :, ps] = (work[k, :, ps] + term) * inv[:, ps]
        return carry

    lax.fori_loop(0, CHUNKS, correct, 0)

    gram = jnp.zeros((kk * 8, kk * 8), F32)
    for g in range(th // 8):
        x, x_rest = two_parts(work[:, pl.ds(g * 8, 8)].reshape(kk * 8, nphi))
        high[g] = x
        low[g] = x_rest
        both = jnp.concatenate([x, x], axis=1)
        gram = gram + dot(both, jnp.concatenate([x, x_rest + x_rest], axis=1), NT)
    gram = lane_sums(group_sums(gram, 8, kk), 8, kk)
    share(1, 0, pack(gram))
    share(1, 1, total(1, 0))
    gram = unpack(total(1, 1)) / cells
    gram_out[...] = 0.5 * (gram + gram.T)

    for c in range(CHUNKS):
        wait_all(send, c, fs_sem)
        wait_all(prod, c, bs_sem)


def basis_kernel(high, low, gram_in, ray_in, basis_out, ray_out, out, out_sem):
    groups, rows, nphi = high.shape
    kk = rows // 8
    part = [pl.ds(8 * g, 8) for g in range(groups)]
    writes = [pltpu.make_async_copy(out.at[:, part[g]], basis_out.at[:, part[g]], out_sem.at[g]) for g in range(groups)]
    ray_out[...] = ray_in[...]

    unit = (iota((kk, kk), 0) == iota((kk, kk), 1)).astype(F32)
    table = jnp.concatenate([gram_in[...], unit], axis=1)
    row = iota(table.shape, 0)
    for first in range(0, kk, 4):
        spread = [jnp.broadcast_to(table[:, j : j + 1], table.shape) for j in range(first, first + 4)]
        for a in range(4):
            j = first + a
            factor = jnp.where(row > j, spread[a] * (1.0 / spread[a][j : j + 1]), 0.0)
            for b in range(a + 1, 4):
                spread[b] = spread[b] - factor * spread[b][j : j + 1]
            table = table - factor * table[j : j + 1]
    scale = jnp.sum(table[:, :kk] * unit, axis=1, keepdims=True)
    factor_inv = table[:, kk:] / jnp.sqrt(scale)

    inv_high, inv_low = two_parts(factor_inv)
    mix_high = block_diagonal(inv_high, 8, False)
    mix_low = block_diagonal(inv_low, 8, False)
    for g in range(groups):
        x = high[g]
        res = dot(mix_high, x) + dot(mix_high, low[g]) + dot(mix_low, x)
        out[:, part[g]] = res.reshape(kk, 8, nphi)
        writes[g].start()
    for copy in writes:
        copy.wait()


def body(vectors, theta_kinetic, potential, phi_coef, centrifugal, coriolis, omega_values):
    kk, _, th, nphi = vectors.shape
    nth = theta_kinetic.shape[0]
    nw, ng = lax.axis_size("omega"), lax.axis_size("grid")
    ny = 4 if ng % 16 == 0 else 2
    nz = ng // ny
    kc = kk // CHUNKS
    cells = nw * nth * nphi
    lanes = kc * PH
    dma = pltpu.SemaphoreType.DMA
    vmem = pltpu.VMEM
    anywhere = pl.BlockSpec(memory_space=pl.ANY)
    local = pl.BlockSpec(memory_space=pltpu.VMEM)
    small = jax.ShapeDtypeStruct((kk, kk), F32)
    blocks = (CHUNKS, ng, th, lanes)
    split = vmem((th // 8, kk * 8, nphi), BF16)
    high, low, gram, rayleigh = pl.pallas_call(
        functools.partial(main_kernel, (nw, ng, ny, nz, cells)),
        out_shape=(split, split, small, small),
        in_specs=[anywhere] * 8,
        out_specs=(local, local, local, local),
        scratch_shapes=[
            vmem((kk, th, nphi), BF16), vmem((nth, nth), BF16), vmem((nphi, nphi), BF16), vmem((th, nphi), F32),
            vmem((1, th), F32), vmem((1, th), F32), vmem((1, th), F32), vmem((1, 1), jnp.int32),
            vmem((512, 512), BF16),
            vmem(blocks, BF16), vmem(blocks, BF16), vmem(blocks, BF16), vmem(blocks, BF16),
            vmem((kk, th, nphi), BF16), vmem((kk, th, nphi), BF16),
            vmem((th, 128), F32), vmem((th, 128), F32),
            vmem((th, nphi), F32), vmem((th, nphi), F32),
            vmem((kk, th, nphi), F32),
            vmem((CHUNKS, kk, lanes), F32),
            vmem((2, nw * ny, 8, 128), F32), vmem((2, nz, 8, 128), F32),
            dma((CHUNKS,)), dma((7,)),
            dma((CHUNKS,)), dma((CHUNKS,)), dma((CHUNKS,)), dma((CHUNKS,)),
            dma((3,)), dma((3,)), dma((2, 2)), dma((2, 2)),
        ],
        compiler_params=pltpu.CompilerParams(
            collective_id=0, has_side_effects=True, vmem_limit_bytes=48 * 1024 * 1024
        ),
    )(
        *(
            pltpu.with_memory_space_constraint(x, pltpu.HBM)
            for x in (
                vectors.reshape(kk, th, nphi),
                theta_kinetic,
                jnp.asarray(phi_table(nphi)),
                potential,
                phi_coef.reshape(1, th),
                centrifugal.reshape(1, th),
                coriolis.reshape(1, th),
            )
        ),
        omega_values.reshape(1, 1),
    )
    basis, rayleigh = pl.pallas_call(
        basis_kernel,
        out_shape=(jax.ShapeDtypeStruct((kk, th, nphi), F32), small),
        in_specs=[local] * 4,
        out_specs=(anywhere, local),
        scratch_shapes=[
            vmem((kk, th, nphi), F32), dma((th // 8,)),
        ],
        compiler_params=pltpu.CompilerParams(vmem_limit_bytes=32 * 1024 * 1024),
    )(high, low, gram, rayleigh)
    return basis.reshape(vectors.shape), rayleigh


def solution(mesh):
    placed = (
        P(None, "omega", "grid", None),
        P(),
        P("grid", None),
        P("grid"),
        P("grid"),
        P("omega", "grid"),
        P("omega"),
    )
    return jax.shard_map(
        body,
        mesh=mesh,
        in_specs=placed,
        out_specs=(P(None, "omega", "grid", None), P()),
        check_vma=False,
    )
```

```python
import functools

import jax
import jax.numpy as jnp
import numpy as np
from jax import lax
from jax.experimental import pallas as pl
from jax.experimental.pallas import tpu as pltpu
from jax.sharding import PartitionSpec as P

JTOT = 7
CHUNKS = 4
PH = 32
HALF = 16
F32 = jnp.float32
BF16 = jnp.bfloat16
MESH = pl.DeviceIdType.MESH
HI = lax.Precision.HIGHEST
NN = (((1,), (0,)), ((), ()))
NT = (((1,), (1,)), ((), ()))
TN = (((0,), (0,)), ((), ()))


def phi_table(count):
    row_idx = np.arange(count, dtype=np.int32)[:, None]
    col_idx = np.arange(count, dtype=np.int32)[None, :]
    offset = (row_idx - col_idx) % count
    parity = (1 - 2 * (offset % 2)).astype(np.float32)
    sine = np.sin(np.float32(np.pi) * offset.astype(np.float32) / np.float32(count)).astype(np.float32)
    safe = np.where(offset == 0, np.float32(1.0), sine * sine)
    off_diag = parity / (np.float32(2.0) * safe)
    centre = np.float32((count * count + 2) / 12.0)
    table = np.where(offset == 0, centre, off_diag) * np.float32(12.0 / (count * count))
    return table.astype(jnp.bfloat16)


def dot(a, b, dims=NN):
    return lax.dot_general(a, b, dims, preferred_element_type=F32)


def exact_dot(a, b, dims=NN):
    return lax.dot_general(a, b, dims, precision=HI, preferred_element_type=F32)


def iota(shape, dim):
    return lax.broadcasted_iota(jnp.int32, shape, dim)


def two_parts(x):
    high = x.astype(BF16)
    return high, (x - high.astype(F32)).astype(BF16)


def as_column(row):
    n = row.shape[1]
    wide = jnp.broadcast_to(row, (n, n))
    return jnp.sum(jnp.where(iota((n, n), 0) == iota((n, n), 1), wide, 0.0), axis=1, keepdims=True)


def group_sums(product, inner, outer):
    rows, cols = product.shape
    kept = jnp.where(iota((rows, cols), 0) % inner == iota((rows, cols), 1) % inner, product, 0.0)
    return jnp.sum(kept.reshape(rows // inner, inner, cols), axis=1)


def lane_sums(x, inner, outer):
    lanes = x.shape[1]
    pick = (iota((lanes, outer), 0) // inner == iota((lanes, outer), 1)).astype(F32)
    return exact_dot(x, pick)


def block_diagonal(small, inner, transposed):
    n = small.shape[0]
    full = n * inner
    rows = (iota((full, n), 0) // inner == iota((full, n), 1)).astype(BF16)
    cols = (iota((n, full), 1) // inner == iota((n, full), 0)).astype(BF16)
    tall = dot(rows, small, NT if transposed else NN).astype(BF16)
    wide = dot(tall, cols)
    same = iota((full, full), 0) % inner == iota((full, full), 1) % inner
    return jnp.where(same, wide, 0.0).astype(BF16)


def pack(x):
    return jnp.concatenate([x[8 * a : 8 * a + 8] for a in range(4)], axis=1)


def unpack(x):
    return jnp.concatenate([x[:, 32 * a : 32 * a + 32] for a in range(4)], axis=0)


def main_kernel(
    sizes,
    v_in, t_in, tab_in, pot_in, pc_in, cf_in, co_in, om_in,
    high, low, gram_out, ray_out,
    vv, tt, tab, pot, pc, cf, co, om,
    perm, send, cols, prod, back, below, above, bond, bond_below, diag, inv, work, racc,
    ar_wy, ar_z,
    v_sem, in_sem, fs_sem, fr_sem, bs_sem, br_sem, ns_sem, nr_sem, as_sem, ar_sem,
):
    nw, ng, ny, nz, cells = sizes
    kk, th, nphi = vv.shape
    kc = kk // CHUNKS
    lanes = kc * PH
    tiles = nphi // 128
    w = lax.axis_index("omega")
    me = lax.axis_index("grid")
    z, y = me // ny, me % ny

    v_copies = [
        pltpu.make_async_copy(v_in.at[pl.ds(c * kc, kc)], vv.at[pl.ds(c * kc, kc)], v_sem.at[c])
        for c in range(CHUNKS)
    ]
    in_copies = [
        pltpu.make_async_copy(src, dst, in_sem.at[i])
        for i, (src, dst) in enumerate(
            ((om_in, om), (co_in, co), (pc_in, pc), (cf_in, cf), (pot_in, pot), (tab_in, tab), (t_in, tt))
        )
    ]
    v_copies[0].start()

    def grid_peer(i):
        return lax.rem(z + i // ny, nz) * ny + lax.rem(y + i % ny, ny)

    barrier = pltpu.get_barrier_semaphore()

    def greet(i, carry):
        pl.semaphore_signal(barrier, inc=1, device_id={"grid": grid_peer(i), "omega": w}, device_id_type=MESH)
        return carry

    lax.fori_loop(1, ng, greet, 0)
    def greet_beside(i, carry):
        peer = {"grid": z * ny + i % ny, "omega": lax.rem(w + i // ny, nw)}
        pl.semaphore_signal(barrier, inc=1, device_id=peer, device_id_type=MESH)
        return carry

    lax.fori_loop(ny, nw * ny, greet_beside, 0)

    for copy in v_copies[1:] + in_copies:
        copy.start()

    source = iota((512, 512), 0)
    target = (source // PH) % 4 * 128 + source // 128 * PH + source % PH
    perm[...] = (target == iota((512, 512), 1)).astype(BF16)

    def to_columns(c):
        spots = [(q, t) for q in range(2) for t in range(tiles)]
        block = vv[pl.ds(c * kc, kc)]
        left = jnp.concatenate(
            [
                jnp.concatenate([block[4 * q + a, :, 128 * t : 128 * t + 128] for a in range(4)], axis=1)
                for q, t in spots
            ],
            axis=0,
        )
        moved = dot(left, perm[...]).astype(BF16)
        for n, (q, t) in enumerate(spots):
            for s in range(4):
                send[c, 4 * t + s, :, 128 * q : 128 * q + 128] = moved[n * th : n * th + th, 128 * s : 128 * s + 128]

    def scatter(c, src, dst, send_sem, recv_sem):
        def one(i, carry):
            peer = grid_peer(i)
            pltpu.make_async_remote_copy(
                src_ref=src.at[c, peer],
                dst_ref=dst.at[c, me],
                send_sem=send_sem.at[c],
                recv_sem=recv_sem.at[c],
                device_id={"grid": peer, "omega": w},
                device_id_type=MESH,
            ).start()
            return carry

        lax.fori_loop(1, ng, one, 0)
        dst[c, me] = src[c, me]

    def wait_all(buf, c, sem):
        rest = buf.at[c, pl.ds(0, ng - 1)]
        pltpu.make_async_copy(rest, rest, sem.at[c]).wait()

    v_copies[0].wait()
    to_columns(0)
    pl.semaphore_wait(barrier, ng - 1 + (nw - 1) * ny)
    scatter(0, send, cols, fs_sem, fr_sem)
    for c in range(1, CHUNKS):
        v_copies[c].wait()

    def next_chunk(c, carry):
        to_columns(c)
        scatter(c, send, cols, fs_sem, fr_sem)
        return carry

    lax.fori_loop(1, CHUNKS, next_chunk, 0)

    for copy in in_copies:
        copy.wait()
    jtotal = F32(JTOT * (JTOT + 1))
    omega = om[...].astype(F32)
    bond_scale = jnp.sqrt(jtotal - omega * (omega + 1.0)) / JTOT
    cent_factor = (jtotal - 2.0 * omega * omega) / jtotal
    bond[...] = jnp.broadcast_to(as_column(co[...]) * bond_scale, (th, 128))
    up = {"grid": me, "omega": lax.rem(w + 1, nw)}
    down = {"grid": me, "omega": lax.rem(w + nw - 1, nw)}
    sides = [
        pltpu.make_async_remote_copy(
            src_ref=src, dst_ref=dst, send_sem=ns_sem.at[i], recv_sem=nr_sem.at[i], device_id=to, device_id_type=MESH
        )
        for i, (src, dst, to) in enumerate(((vv, below, up), (vv, above, down), (bond, bond_below, up)))
    ]
    for copy in sides:
        copy.start()

    diag[...] = pot[...] + cent_factor * as_column(cf[...])
    inv[...] = 1.0 / (1.0 + pot[...])
    phi_scale = as_column(pc[...])
    wide = min(256, nphi)

    def local_terms(i, carry):
        ks = pl.ds(i // (nphi // wide) * kc, kc)
        ps = pl.ds(pl.multiple_of(i % (nphi // wide) * wide, wide), wide)
        term = dot(vv[ks].reshape(kc * th, nphi), tab[:, ps]).reshape(kc, th, wide)
        work[ks, :, ps] = term * phi_scale[None] + diag[:, ps][None] * vv[ks, :, ps].astype(F32)
        return carry

    lax.fori_loop(0, CHUNKS * (nphi // wide), local_terms, 0)

    def theta_product(c):
        wait_all(cols, c, fr_sem)
        block = cols[c].reshape(ng * th, lanes)
        part = ng // 4

        def rows(i, carry):
            out = dot(tt[pl.ds(i * part * th, part * th)], block).astype(BF16)
            prod[c, pl.ds(i * part, part)] = out.reshape(part, th, lanes)
            return carry

        lax.fori_loop(0, 4, rows, 0)

    def ray_columns(c):
        def pair(i, carry):
            a = jnp.where(i <= c, c, i - c - 1)
            b = jnp.where(i <= c, i, c)
            product = dot(cols[a].reshape(ng * th, lanes), prod[b].reshape(ng * th, lanes), TN)
            racc[b, pl.ds(a * kc, kc)] = group_sums(product, PH, kc)
            return carry

        lax.fori_loop(0, 2 * c + 1, pair, 0)

    theta_product(0)
    scatter(0, prod, back, bs_sem, br_sem)
    ray_columns(0)
    theta_product(1)
    ray_columns(1)

    for copy in sides:
        copy.wait()
    above_factor = jnp.where(w < nw - 1, bond[...], 0.0)[:, :1]
    below_factor = jnp.where(w > 0, bond_below[...], 0.0)[:, :1]

    def couple(i, carry):
        ks = pl.ds(i * 4, 4)
        work[ks] = work[ks] + above_factor[None] * above[ks].astype(F32) + below_factor[None] * below[ks].astype(F32)
        return carry

    lax.fori_loop(0, kk // 4, couple, 0)

    theta_product(2)
    ray_columns(2)

    ray = jnp.zeros((kk, kk), F32)
    for h in range(th // HALF):
        rows = pl.ds(h * HALF, HALF)
        left = vv[:, rows].reshape(kk * HALF, nphi)
        x, x_rest = two_parts(work[:, rows].reshape(kk * HALF, nphi))
        ray = ray + lane_sums(group_sums(dot(left, x, NT) + dot(left, x_rest, NT), HALF, kk), HALF, kk)

    theta_product(3)
    ray_columns(3)

    stages = (
        (ar_wy, nw * ny, w * ny + y, lambda i: {"grid": z * ny + i % ny, "omega": i // ny}),
        (ar_z, nz, z, lambda i: {"grid": i * ny + y, "omega": w}),
    )

    def share(a, s, value):
        buf, n, mine, device = stages[s]
        buf[a, mine] = value

        def one(i, carry):
            pltpu.make_async_remote_copy(
                src_ref=buf.at[a, mine],
                dst_ref=buf.at[a, mine],
                send_sem=as_sem.at[a, s],
                recv_sem=ar_sem.at[a, s],
                device_id=device(lax.rem(mine + i, n)),
                device_id_type=MESH,
            ).start()
            return carry

        lax.fori_loop(1, n, one, 0)

    def total(a, s):
        buf, n, _, _ = stages[s]
        rest = buf.at[a, pl.ds(0, n - 1)]
        pltpu.make_async_copy(rest, rest, ar_sem.at[a, s]).wait()
        pltpu.make_async_copy(rest, rest, as_sem.at[a, s]).wait()
        return jnp.sum(buf[a], axis=0)

    ray_cols = jnp.concatenate([racc[b] for b in range(CHUNKS)], axis=1)
    ray = ray + lane_sums(ray_cols, PH, kk)
    share(0, 0, pack(ray))
    scatter(1, prod, back, bs_sem, br_sem)
    share(0, 1, total(0, 0))
    scatter(2, prod, back, bs_sem, br_sem)
    ray = unpack(total(0, 1)) / cells
    scatter(3, prod, back, bs_sem, br_sem)
    ray_out[...] = ray

    ray_high, ray_low = two_parts(ray)
    mix_high = block_diagonal(ray_high, HALF, True)
    mix_low = block_diagonal(ray_low, HALF, True)

    def project(i, carry):
        rows = pl.ds(pl.multiple_of(i // (nphi // wide) * HALF, HALF), HALF)
        ps = pl.ds(pl.multiple_of(i % (nphi // wide) * wide, wide), wide)
        right = vv[:, rows, ps].reshape(kk * HALF, wide)
        taken = (dot(mix_high, right) + dot(mix_low, right)).reshape(kk, HALF, wide)
        work[:, rows, ps] = work[:, rows, ps] - taken
        return carry

    lax.fori_loop(0, th // HALF * (nphi // wide), project, 0)

    def correct(c, carry):
        wait_all(back, c, br_sem)
        spots = [(q, t) for q in range(2) for t in range(tiles)]
        left = jnp.concatenate(
            [
                jnp.concatenate([back[c, 4 * t + s, :, 128 * q : 128 * q + 128] for s in range(4)], axis=1)
                for q, t in spots
            ],
            axis=0,
        )
        theta = dot(left, perm[...])
        for n, (q, t) in enumerate(spots):
            ps = slice(128 * t, 128 * t + 128)
            done = []
            for a in range(4):
                term = theta[n * th : n * th + th, 128 * a : 128 * a + 128]
                done.append((work[c * kc + 4 * q + a, :, ps] + term) * inv[:, ps])
            for a in (0, 2):
                rows = pl.ds(pl.multiple_of((c * kc + 4 * q + a) * 8, 16), 16)
                for g in range(th // 8):
                    pair = jnp.concatenate([d[8 * g : 8 * g + 8] for d in done[a : a + 2]], axis=0)
                    high[g, rows, ps], low[g, rows, ps] = two_parts(pair)
        return carry

    lax.fori_loop(0, CHUNKS, correct, 0)

    gram = jnp.zeros((kk * 8, kk * 8), F32)
    cross = jnp.zeros((kk * 8, kk * 8), F32)
    for g in range(th // 8):
        gram = gram + dot(high[g], high[g], NT)
        cross = cross + dot(high[g], low[g], NT)
    gram = gram + cross + cross
    gram = lane_sums(group_sums(gram, 8, kk), 8, kk)
    share(1, 0, pack(gram))
    share(1, 1, total(1, 0))
    gram = unpack(total(1, 1)) / cells
    gram_out[...] = 0.5 * (gram + gram.T)

    for c in range(CHUNKS):
        wait_all(send, c, fs_sem)
        wait_all(prod, c, bs_sem)


def basis_kernel(high, low, gram_in, ray_in, basis_out, ray_out, out, out_sem):
    groups, rows, nphi = high.shape
    kk = rows // 8
    ray_out[...] = ray_in[...]

    unit = (iota((kk, kk), 0) == iota((kk, kk), 1)).astype(F32)
    table = jnp.concatenate([gram_in[...], unit], axis=1)
    row = iota(table.shape, 0)
    for first in range(0, kk, 16):
        spread = [jnp.broadcast_to(table[:, j : j + 1], table.shape) for j in range(first, first + 16)]
        for a in range(16):
            j = first + a
            factor = jnp.where(row > j, spread[a] * (1.0 / spread[a][j : j + 1]), 0.0)
            for b in range(a + 1, 16):
                spread[b] = spread[b] - factor * spread[b][j : j + 1]
            table = table - factor * table[j : j + 1]
    scale = jnp.sum(table[:, :kk] * unit, axis=1, keepdims=True)
    factor_inv = table[:, kk:] / jnp.sqrt(scale)

    inv_high, inv_low = two_parts(factor_inv)
    mix_high = block_diagonal(inv_high, 8, False)
    mix_low = block_diagonal(inv_low, 8, False)
    writes = []
    wide = nphi // 2
    for g in range(groups):
        for t in range(2):
            ps = slice(t * wide, t * wide + wide)
            part = slice(8 * g, 8 * g + 8)
            x = high[g, :, ps]
            res = dot(mix_high, x) + dot(mix_high, low[g, :, ps]) + dot(mix_low, x)
            out[:, part, ps] = res.reshape(kk, 8, wide)
            copy = pltpu.make_async_copy(out.at[:, part, ps], basis_out.at[:, part, ps], out_sem.at[len(writes)])
            copy.start()
            writes.append(copy)
    for copy in writes:
        copy.wait()


def body(vectors, theta_kinetic, potential, phi_coef, centrifugal, coriolis, omega_values):
    kk, _, th, nphi = vectors.shape
    nth = theta_kinetic.shape[0]
    nw, ng = lax.axis_size("omega"), lax.axis_size("grid")
    ny = 4 if ng % 16 == 0 else 2
    nz = ng // ny
    kc = kk // CHUNKS
    cells = nw * nth * nphi
    lanes = kc * PH
    dma = pltpu.SemaphoreType.DMA
    vmem = pltpu.VMEM
    anywhere = pl.BlockSpec(memory_space=pl.ANY)
    local = pl.BlockSpec(memory_space=pltpu.VMEM)
    small = jax.ShapeDtypeStruct((kk, kk), F32)
    blocks = (CHUNKS, ng, th, lanes)
    split = vmem((th // 8, kk * 8, nphi), BF16)
    high, low, gram, rayleigh = pl.pallas_call(
        functools.partial(main_kernel, (nw, ng, ny, nz, cells)),
        out_shape=(split, split, small, small),
        in_specs=[anywhere] * 8,
        out_specs=(local, local, local, local),
        scratch_shapes=[
            vmem((kk, th, nphi), BF16), vmem((nth, nth), BF16), vmem((nphi, nphi), BF16), vmem((th, nphi), F32),
            vmem((1, th), F32), vmem((1, th), F32), vmem((1, th), F32), vmem((1, 1), jnp.int32),
            vmem((512, 512), BF16),
            vmem(blocks, BF16), vmem(blocks, BF16), vmem(blocks, BF16), vmem(blocks, BF16),
            vmem((kk, th, nphi), BF16), vmem((kk, th, nphi), BF16),
            vmem((th, 128), F32), vmem((th, 128), F32),
            vmem((th, nphi), F32), vmem((th, nphi), F32),
            vmem((kk, th, nphi), F32),
            vmem((CHUNKS, kk, lanes), F32),
            vmem((2, nw * ny, 8, 128), F32), vmem((2, nz, 8, 128), F32),
            dma((CHUNKS,)), dma((7,)),
            dma((CHUNKS,)), dma((CHUNKS,)), dma((CHUNKS,)), dma((CHUNKS,)),
            dma((3,)), dma((3,)), dma((2, 2)), dma((2, 2)),
        ],
        compiler_params=pltpu.CompilerParams(
            collective_id=0, has_side_effects=True, vmem_limit_bytes=48 * 1024 * 1024
        ),
    )(
        *(
            pltpu.with_memory_space_constraint(x, pltpu.HBM)
            for x in (
                vectors.reshape(kk, th, nphi),
                theta_kinetic,
                jnp.asarray(phi_table(nphi)),
                potential,
                phi_coef.reshape(1, th),
                centrifugal.reshape(1, th),
                coriolis.reshape(1, th),
            )
        ),
        omega_values.reshape(1, 1),
    )
    basis, rayleigh = pl.pallas_call(
        basis_kernel,
        out_shape=(jax.ShapeDtypeStruct((kk, th, nphi), F32), small),
        in_specs=[local] * 4,
        out_specs=(anywhere, local),
        scratch_shapes=[
            vmem((kk, th, nphi), F32), dma((th // 4,)),
        ],
        compiler_params=pltpu.CompilerParams(vmem_limit_bytes=32 * 1024 * 1024),
    )(high, low, gram, rayleigh)
    return basis.reshape(vectors.shape), rayleigh


def solution(mesh):
    placed = (
        P(None, "omega", "grid", None),
        P(),
        P("grid", None),
        P("grid"),
        P("grid"),
        P("omega", "grid"),
        P("omega"),
    )
    return jax.shard_map(
        body,
        mesh=mesh,
        in_specs=placed,
        out_specs=(P(None, "omega", "grid", None), P()),
        check_vma=False,
    )
```
